32 devices in a mesh: section: 2 (over x), dp: 4 (over y, core), tensor: 4 (over z).
Axes of the slice: x: 2, y: 2, z: 4, core: 2. Of those that a mesh axis runs over, the one named last changes fastest.
Arguments:
- incoming: bfloat16 [2, 3, 256, 8192], P('section', None, ('dp', 'tensor')), may hold values from -6 to 6
- hidden: bfloat16 [2, 3, 256, 8192], P('section', None, ('dp', 'tensor')), may hold values from -6 to 6
- expert_out: bfloat16 [2, 3, 256, 2, 8192], P('section', None, ('dp', 'tensor')), may hold values from -0.59765625 to 0.59765625
- routes: int32 [2, 3, 256, 2], P('section', None, ('dp', 'tensor')), may hold values from 0 to 3, all different within a row; in each aligned block of 16 rows (0 to 15, 16 to 31, ..., all dimensions but the last counted through in order) at most 16 rows name the same one
- expert_back: bfloat16 [2, 3, 1024, 8192], P('section', None, ('dp', 'tensor')), may hold values from -0.59765625 to 0.59765625
- scan_out: bfloat16 [2, 3, 256, 8192], P('section', None, 'dp', 'tensor'), may hold values from -6 to 6
- gate_in: bfloat16 [2, 3, 256, 8192], P('section', None, 'dp', 'tensor'), may hold values from -9 to 9
- w_out: bfloat16 [2, 8192, 8192], P('section', 'tensor'), may hold values from -0.0625 to 0.0625
- w_router: bfloat16 [2, 8192, 4], P('section', 'dp'), may hold values from -0.0625 to 0.0625
- norm_gain: bfloat16 [2, 8192], P('section', 'dp'), may hold values from 0.5 to 1.5
Outputs:
- passed: bfloat16 [2, 3, 256, 8192], P('section', None, ('dp', 'tensor'))
- scan_grad: bfloat16 [2, 3, 256, 8192], P('section', None, 'dp', 'tensor')
- gate_grad: bfloat16 [2, 3, 256, 8192], P('section', None, 'dp', 'tensor')
- expert_grad: bfloat16 [2, 3, 1024, 8192], P('section', None, ('dp', 'tensor'))
- w_out_grad: float32 [2, 8192, 8192], P('section', 'tensor', 'dp')
- router_grad: float32 [2, 8192, 4], P('section', 'dp')
- gain_grad: float32 [2, 8192], P('section', 'dp')
The draws below stay inside these ranges and needn't reach their ends.
Inputs may be any that keep to these rules, and one draw needn't show every extreme that they name: `routes`: each row names 2 different experts. In each aligned block of 16 rows (the rows of one device) no expert is named by more than 16 rows, a bound that some block reaches.
All inputs are finite; a program needn't handle non-finite values.
Results may differ from the reference program's by a relative error of at most 0.025.
Values may be sent and summed in bfloat16 or wider, within the bound.
No kernel may reach another device: no remote copies, remote signals or barrier semaphores. Data moves between devices by JAX's collectives and lax.ppermute only.
A program may use at most 320 MiB of HBM per device.

```python
import math
import jax
import jax.numpy as jnp
import numpy as np
from jax import lax

D = 8192
DI = 8192
TOPK = 2
TOK_DEV = 16
MICRO = 3
EXPERTS = 4
CAP = 16
GROUP = 64
TOKENS = 256
SLOT_ROWS = 1024
N_DP = 4
N_TENSOR = 4


def steps_of(rng, extent, split, low, high):
    def one(dim, blocks):
        heights = jax.random.uniform(jax.random.fold_in(jax.random.fold_in(rng, 6), dim), (blocks,), jnp.float32, low / len(split), high / len(split))
        return jnp.repeat(jnp.exp(heights), extent[dim] // blocks).reshape((-1,) + (1,) * (len(extent) - dim - 1))

    level = one(*split[0])
    for cut in split[1:]:
        level = level * one(*cut)
    return level


def assign_block(stream_key, own, number, rows, count, top, bound, skew):
    ranking = jax.random.permutation(stream_key, count)
    packed, ordinary = portions_of(count, rows * top, bound, skew, True), portions_of(count, rows * top, bound, skew, False)
    places = jnp.arange(count)

    def named(tallies, turn):
        used = int((tallies > 0).sum())
        fixed = max(1, used // 4)
        moved = fixed + (places - fixed + turn * (used - fixed)) % max(1, count - fixed)
        return jnp.zeros((count,), jnp.int32).at[ranking[jnp.where(places < fixed, places, moved)]].set(jnp.asarray(tallies, jnp.int32))

    tallies = jnp.where(number % 4 == 0, named(packed, number // 4), named(ordinary, number - number // 4 - 1))
    mixed = jax.random.permutation(jax.random.fold_in(own, 3), count)
    donor, receiver = mixed[0:count // 2 * 2:2], mixed[1:count // 2 * 2:2]
    slack = jnp.minimum(tallies[donor] - 1, bound - tallies[receiver]) // 2
    slack = jnp.where((donor == ranking[0]) | (receiver == ranking[0]) | (tallies[receiver] == 0), 0, jnp.maximum(slack, 0))
    moved = jax.random.randint(jax.random.fold_in(own, 4), (count // 2,), 0, 1 << 20) % (slack + 1)
    tallies = tallies.at[donor].add(-moved).at[receiver].add(moved)
    members = jnp.searchsorted(jnp.cumsum(tallies), jnp.arange(rows * top), side="right").astype(jnp.int32)
    table = members.reshape(top, rows).T
    table = table[jax.random.permutation(jax.random.fold_in(own, 1), rows)]
    turn = jax.random.randint(jax.random.fold_in(own, 2), (rows, 1), 0, top)
    return jnp.take_along_axis(table, (jnp.arange(top)[None, :] + turn) % top, axis=1)


def portions_of(number_of, total, most, skew, full):
    portions = [(1 << 20) // math.isqrt(grade ** skew) + 1 for grade in range(1, number_of + 1)]
    largest = most if full else min(most, max(-(-total // number_of), total * portions[0] // sum(portions)))
    least = 1 if total - largest >= number_of - 1 else 0
    given, rest = [largest] + [least] * (number_of - 1), total - largest - least * (number_of - 1)
    while rest > 0:
        candidates = [i for i in range(1, number_of) if given[i] < largest] or [i for i in range(1, number_of) if given[i] < most]
        mass, left = sum([portions[i] for i in candidates]), rest
        for i in candidates:
            extra = min(most - given[i], max(1, left * portions[i] // mass), rest)
            given[i] = given[i] + extra
            rest = rest - extra
    return np.array(given)


def scatter_about(key, shape, deviation, reach, shards=(), kind=jnp.bfloat16):
    result = deviation * jax.random.normal(key, shape, jnp.float32)
    if shards:
        result = result * steps_of(key, shape, shards, -0.22, 0.18)
    return jnp.clip(result, -reach, reach).astype(kind)


def setup_inputs(seed: int = 0) -> dict:
    seeds = jax.random.split(jax.random.key(seed), 11)
    incoming = scatter_about(seeds[0], (2, MICRO, TOKENS, D), 1.0, 6.0, ((0, 2), (2, 16)))
    hidden = scatter_about(seeds[1], (2, MICRO, TOKENS, D), 1.0, 6.0, ((0, 2), (2, 16)))
    expert_out = scatter_about(seeds[2], (2, MICRO, TOKENS, TOPK, D), 0.1, 0.59765625, ((0, 2), (2, 16)))
    routes_keys = jax.random.split(jax.random.fold_in(seeds[3], 1), 2 * MICRO * TOKENS // TOK_DEV)
    routes_turns = jax.random.permutation(jax.random.fold_in(seeds[3], 3), 2 * MICRO * TOKENS // TOK_DEV)
    routes = jax.vmap(lambda own, number: assign_block(jax.random.fold_in(seeds[3], 2), own, number, TOK_DEV, EXPERTS, TOPK, CAP, 2))(routes_keys, routes_turns).reshape((2, MICRO, TOKENS, TOPK))
    expert_back = scatter_about(seeds[4], (2, MICRO, SLOT_ROWS, D), 0.1, 0.59765625, ((0, 2), (2, 16)))
    scan_out = scatter_about(seeds[5], (2, MICRO, TOKENS, DI), 1.0, 6.0, ((0, 2), (2, 4), (3, 4)))
    gate_in = scatter_about(seeds[6], (2, MICRO, TOKENS, DI), 1.5, 9.0, ((0, 2), (2, 4), (3, 4)))
    w_out = scatter_about(seeds[7], (2, DI, D), DI ** -0.5, 0.0625, ((0, 2), (1, 4)))
    w_router = scatter_about(seeds[8], (2, D, EXPERTS), D ** -0.5, 0.0625, ((0, 2), (1, 4)))
    norm_gain = jnp.clip(1.0 + 0.1 * jax.random.normal(seeds[9], (2, D), jnp.float32), 0.5, 1.5).astype(jnp.bfloat16)
    return {"incoming": incoming, "hidden": hidden, "expert_out": expert_out, "routes": routes, "expert_back": expert_back, "scan_out": scan_out, "gate_in": gate_in, "w_out": w_out, "w_router": w_router, "norm_gain": norm_gain}


def slot_rows(route_ids):
    blocks = TOKENS // TOK_DEV
    flat_ids = route_ids.reshape(blocks, TOK_DEV * TOPK)
    onehot = (flat_ids[:, :, None] == jnp.arange(EXPERTS, dtype=jnp.int32)[None, None, :]).astype(jnp.int32)
    before = jnp.cumsum(onehot, axis=1, dtype=jnp.int32) - onehot
    slot_index = lax.optimization_barrier(jnp.sum(before * onehot, axis=2, dtype=jnp.int32))
    block_ids = jnp.arange(blocks, dtype=jnp.int32)[:, None]
    data_group = block_ids // N_TENSOR
    position = block_ids % N_TENSOR
    return (((data_group * EXPERTS + flat_ids) * N_TENSOR + position) * CAP + slot_index).reshape(-1)

def moe_backward(upstream, hidden_rows, expert_rows, route_ids, back_rows, router, gain):
    hidden_f = hidden_rows.astype(jnp.float32)
    inv_rms = 1.0 / jnp.sqrt(lax.optimization_barrier(jnp.mean(hidden_f * hidden_f, axis=1, keepdims=True)) + 1e-05)
    gain_f = gain.astype(jnp.float32)
    normed = (hidden_f * inv_rms * gain_f).astype(jnp.bfloat16)
    logits = jnp.dot(normed, router, preferred_element_type=jnp.float32)
    weights = jnp.exp(logits)
    route_probs = weights / lax.optimization_barrier(jnp.sum(weights, axis=1, keepdims=True))
    chosen = (route_ids[:, :, None] == jnp.arange(EXPERTS, dtype=jnp.int32)[None, None, :]).astype(jnp.float32)
    route_prob = lax.optimization_barrier(jnp.sum(chosen * route_probs[:, None, :], axis=2))
    upstream_f = upstream.astype(jnp.float32)
    score_grad = jnp.einsum('td,tkd->tk', upstream_f, expert_rows.astype(jnp.float32))
    prob_grad = lax.optimization_barrier(jnp.sum(chosen * score_grad[:, :, None], axis=1))
    logit_grad = (route_probs * (prob_grad - lax.optimization_barrier(jnp.sum(route_probs * prob_grad, axis=1, keepdims=True)))).astype(jnp.bfloat16)
    row_index = slot_rows(route_ids)
    returned = back_rows[row_index].astype(jnp.float32).reshape(TOKENS, TOPK, D)
    norm_grad = jnp.dot(logit_grad, router.T, preferred_element_type=jnp.float32) + lax.optimization_barrier(jnp.sum(returned, axis=1))
    scaled = norm_grad * gain_f
    hidden_grad = inv_rms * scaled - hidden_f * inv_rms ** 3 * lax.optimization_barrier(jnp.mean(scaled * hidden_f, axis=1, keepdims=True))
    passed = (upstream_f + hidden_grad).astype(jnp.bfloat16)
    sent = (route_prob[:, :, None] * upstream_f[:, None, :]).astype(jnp.bfloat16).reshape(TOKENS * TOPK, D)
    expert_grad = jnp.zeros((SLOT_ROWS, D), jnp.bfloat16).at[row_index].set(sent)
    gain_term = lax.optimization_barrier(jnp.sum(norm_grad * hidden_f * inv_rms, axis=0))
    router_term = lax.dot_general(normed, logit_grad, (((0,), (0,)), ((), ())), preferred_element_type=jnp.float32)
    return (passed, expert_grad, gain_term, router_term)

def mixer_backward(passed, scan_rows, gate_rows, weight):
    scan_f = scan_rows.astype(jnp.float32)
    gate_f = gate_rows.astype(jnp.float32)
    sigmoid_gate = jax.nn.sigmoid(gate_f)
    gated = (scan_f * gate_f * sigmoid_gate).astype(jnp.bfloat16)
    inner_grad = lax.dot_general(passed, weight, (((1,), (1,)), ((), ())), preferred_element_type=jnp.float32)
    scan_grad = (inner_grad * gate_f * sigmoid_gate).astype(jnp.bfloat16)
    gate_grad = (inner_grad * scan_f * sigmoid_gate * (1.0 + gate_f * (1.0 - sigmoid_gate))).astype(jnp.bfloat16)
    return (gated, scan_grad, gate_grad)

def reference(incoming, hidden, expert_out, routes, expert_back, scan_out, gate_in, w_out, w_router, norm_gain):
    passed_all = [[], []]
    expert_all = [[], []]
    scan_all = [[], []]
    gate_all = [[], []]
    weight_all = [None, None]
    router_all = [None, None]
    gain_all = [None, None]
    for section_index in (1, 0):
        gain_total = jnp.zeros((D,), jnp.float32)
        router_total = jnp.zeros((D, EXPERTS), jnp.float32)
        gated_list = []
        for micro_step in range(MICRO):
            if section_index == 1 or micro_step == 0:
                upstream = incoming[section_index, micro_step]
            else:
                upstream = passed_all[1][micro_step - 1]
            passed, expert_grad, gain_term, router_term = moe_backward(upstream, hidden[section_index, micro_step], expert_out[section_index, micro_step], routes[section_index, micro_step], expert_back[section_index, micro_step], w_router[section_index], norm_gain[section_index])
            gain_total = gain_total + gain_term
            router_total = router_total + router_term
            gated, scan_grad, gate_grad = mixer_backward(passed, scan_out[section_index, micro_step], gate_in[section_index, micro_step], w_out[section_index])
            passed_all[section_index].append(passed)
            expert_all[section_index].append(expert_grad)
            scan_all[section_index].append(scan_grad)
            gate_all[section_index].append(gate_grad)
            gated_list.append(gated)
        weight_total = jnp.zeros((DI, D), jnp.float32)
        for data_group in range(N_DP):
            first_row = data_group * GROUP
            partial_sum = jnp.zeros((DI, D), jnp.float32)
            for micro_step in range(MICRO):
                gated_rows = gated_list[micro_step][first_row:first_row + GROUP]
                passed_rows = passed_all[section_index][micro_step][first_row:first_row + GROUP]
                partial_sum = partial_sum + lax.dot_general(gated_rows, passed_rows, (((0,), (0,)), ((), ())), preferred_element_type=jnp.float32)
            weight_total = weight_total + lax.optimization_barrier(partial_sum.astype(jnp.bfloat16)).astype(jnp.float32)
        weight_all[section_index] = weight_total
        router_all[section_index] = router_total
        gain_all[section_index] = gain_total
    passed_out = jnp.stack([jnp.stack(passed_all[0]), jnp.stack(passed_all[1])])
    scan_grad_out = jnp.stack([jnp.stack(scan_all[0]), jnp.stack(scan_all[1])])
    gate_grad_out = jnp.stack([jnp.stack(gate_all[0]), jnp.stack(gate_all[1])])
    expert_grad_out = jnp.stack([jnp.stack(expert_all[0]), jnp.stack(expert_all[1])])
    weight_out = jnp.stack(weight_all)
    router_out = jnp.stack(router_all)
    gain_out = jnp.stack(gain_all)
    return (passed_out, scan_grad_out, gate_grad_out, expert_grad_out, weight_out, router_out, gain_out)
```

```python
import jax
import jax.numpy as jnp
from jax import lax
from jax.sharding import PartitionSpec as P

F32 = jnp.float32
BF16 = jnp.bfloat16


def partner(shard, axis, mask):
    length = lax.axis_size(axis)
    return lax.ppermute(shard, axis, [(i, i ^ mask) for i in range(length)])


def around(shard, axis, by):
    length = lax.axis_size(axis)
    return lax.ppermute(shard, axis, [(i, (i + by) % length) for i in range(length)])


def exchange_rows(block, axis):
    length = lax.axis_size(axis)
    got = [around(block, axis, length - r) for r in range(1, length)]
    return [block] + got


def line_gather(block, only_section=None):
    length = lax.axis_size("tensor")
    if length > 4:
        return exchange_rows(block, "tensor")
    me = lax.axis_index("tensor")
    if only_section is None:
        axes, base = "tensor", 0
    else:
        axes, base = ("section", "tensor"), only_section * length
    up, down = block, block
    ups, downs = [], []
    for s in range(1, length):
        up = lax.ppermute(up, axes, [(base + i, base + i + 1) for i in range(s - 1, length - 1)])
        down = lax.ppermute(down, axes, [(base + i, base + i - 1) for i in range(1, length - s + 1)])
        ups.append(up)
        downs.append(down)
    got = [block]
    for r in range(1, length):
        got.append(jnp.where(me + r < length, downs[r - 1], ups[length - r - 1]))
    return got


def turned(blocks, start):
    length = blocks.shape[0]
    twice = jnp.concatenate([blocks, blocks], axis=0)
    return lax.dynamic_slice_in_dim(twice, start, length, axis=0)


def earlier(named):
    count = named.shape[-1]
    order = jnp.arange(count, dtype=jnp.int32)
    before = (order[:, None] < order[None, :]).astype(F32)
    return jnp.sum(named[..., :, None] * before, axis=-2)


def on_device(
    incoming, hidden, expert_out, routes, expert_back, scan_out, gate_in, w_out, w_router, norm_gain
):
    micro = incoming.shape[1]
    rows = incoming.shape[2]
    width = incoming.shape[3]
    experts = w_router.shape[2]
    n = lax.axis_size("tensor")
    n_dp = lax.axis_size("dp")
    cap = expert_back.shape[2] // n
    inner = scan_out.shape[3]
    group = scan_out.shape[2]
    columns = width // n_dp
    me = lax.axis_index("tensor")
    me_dp = lax.axis_index("dp")
    upper = lax.axis_index("section") == 1
    weight = w_out[0]

    def tied(value, *others):
        return lax.optimization_barrier((value,) + others)[0]

    back = expert_back[0].reshape(micro, n, cap, width)
    returned = [lax.dynamic_index_in_dim(back, me, 1, False)]
    for r in range(1, n):
        s = n - r
        block = lax.dynamic_index_in_dim(back, (me + s) % n, 1, False)
        returned.append(around(block, "tensor", s))

    small = jnp.concatenate([w_router[0].T, norm_gain[0][None]], axis=0)
    smalls = jnp.stack([small] + [partner(small, "dp", m) for m in range(1, n_dp)])
    smalls = jnp.stack([lax.dynamic_index_in_dim(smalls, me_dp ^ g, 0, False) for g in range(n_dp)])
    smalls = jnp.swapaxes(smalls, 0, 1).reshape(experts + 1, width)
    router = smalls[:experts]
    gain = smalls[experts:].astype(F32)

    scan_f = scan_out[0].astype(F32)
    gate_f = gate_in[0].astype(F32)
    sig = jax.nn.sigmoid(gate_f)
    gated = (scan_f * gate_f * sig).astype(BF16)
    gated = turned(jnp.swapaxes(gated.reshape(micro, n, rows, inner), 0, 1), me)
    gated = jnp.swapaxes(gated, 0, 1).reshape(micro * group, inner)
    if n_dp == 4:
        across = partner(gated, "dp", 2)
        pair = partner(jnp.stack([gated, across]), "dp", 1)
        gated_all = [gated, pair[0], across, pair[1]]
    else:
        gated_all = [gated] + [partner(gated, "dp", m) for m in range(1, n_dp)]

    hidden_f = hidden[0].astype(F32)
    inv_rms = 1.0 / jnp.sqrt(jnp.mean(hidden_f * hidden_f, axis=2, keepdims=True) + 1e-05)
    normed = (hidden_f * inv_rms * gain).astype(BF16)
    logits = lax.dot_general(
        normed, router, (((2,), (1,)), ((), ())), preferred_element_type=F32
    )
    weights = jnp.exp(logits)
    probs = weights / jnp.sum(weights, axis=2, keepdims=True)
    chosen = (routes[0][..., None] == jnp.arange(experts, dtype=jnp.int32)).astype(F32)
    named = jnp.sum(chosen, axis=2)
    marked = jnp.where(named > 0, probs, -1.0)
    marks = jnp.stack(exchange_rows(marked, "tensor"))

    named_t = jnp.swapaxes(named, 1, 2)
    place = earlier(named_t)
    slots = jnp.arange(cap, dtype=F32)
    pick = named_t[..., None] * (place[..., None] == slots)
    pick = turned(jnp.swapaxes(pick, 0, 1), me)
    pick = jnp.transpose(pick, (1, 2, 0, 3)).reshape(micro, rows, n * cap).astype(BF16)

    mine = lax.dynamic_index_in_dim(marks, me, 3, False)
    mine = jnp.swapaxes(mine, 0, 1)
    mine_named = (mine >= 0).astype(F32)
    mine_place = earlier(mine_named)
    put = mine_named[..., None] * (mine_place[..., None] == slots)
    slot_prob = jnp.sum(put * mine[..., None], axis=2)
    owner = (me + jnp.arange(n, dtype=jnp.int32)) % n
    at = (jnp.arange(n, dtype=jnp.int32)[:, None] == owner[None, :]).astype(F32)
    put = jnp.einsum("jr,mric->mjcri", at, put).reshape(micro, n * cap, n * rows).astype(BF16)
    slot_prob = jnp.einsum("jr,mrc->mjc", at, slot_prob).reshape(micro, n * cap, 1)

    back_sum = jnp.stack(
        [
            jnp.dot(
                pick[t],
                jnp.concatenate([x[t] for x in returned], axis=0),
                preferred_element_type=F32,
            )
            for t in range(micro)
        ]
    )

    def step_back(t0, t1, upstream):
        upstream_f = upstream.astype(F32)
        score = jnp.sum(upstream_f[:, :, None, :] * expert_out[0, t0:t1].astype(F32), axis=3)
        prob_grad = jnp.sum(chosen[t0:t1] * score[..., None], axis=2)
        p = probs[t0:t1]
        logit_grad = (p * (prob_grad - jnp.sum(p * prob_grad, axis=2, keepdims=True))).astype(BF16)
        norm_grad = back_sum[t0:t1] + lax.dot_general(
            logit_grad, router, (((2,), (0,)), ((), ())), preferred_element_type=F32
        )
        h = hidden_f[t0:t1]
        inv = inv_rms[t0:t1]
        scaled = norm_grad * gain
        hidden_grad = inv * scaled - h * inv**3 * jnp.mean(scaled * h, axis=2, keepdims=True)
        passed = (upstream_f + hidden_grad).astype(BF16)
        return passed, logit_grad, norm_grad

    first, logit_first, norm_first = step_back(0, micro, incoming[0])
    received = lax.ppermute(first[: micro - 1], "section", [(1, 0)])
    gathered = [jnp.concatenate(line_gather(first[0]), axis=0)]
    later_up = jnp.where(upper, incoming[0, 1:], received)
    later, logit_later, norm_later = step_back(1, micro, later_up)
    passed_all = jnp.concatenate([first[:1], later], axis=0)
    for t in range(1, micro):
        gathered.append(jnp.concatenate(line_gather(later[t - 1]), axis=0))
    sources = []
    for t in range(micro):
        rows_in = tied(incoming[0, t], gathered[micro - 1])
        sources.append(jnp.concatenate(line_gather(rows_in), axis=0))
    for t in range(1, micro):
        above = lax.ppermute(gathered[t - 1], "section", [(1, 0)])
        sources[t] = jnp.where(upper, sources[t], above)

    logit_grads = jnp.concatenate([logit_first[:1], logit_later], axis=0)
    norm_grads = jnp.concatenate([norm_first[:1], norm_later], axis=0)
    router_term = lax.dot_general(
        logit_grads.reshape(micro * rows, experts),
        normed.reshape(micro * rows, width),
        (((0,), (0,)), ((), ())),
        preferred_element_type=F32,
    )
    gain_term = jnp.sum(norm_grads * hidden_f * inv_rms, axis=(0, 1))[None]
    term = jnp.concatenate([router_term, gain_term], axis=0)
    total = lax.dynamic_slice_in_dim(term, me_dp * columns, columns, axis=1)
    for m in range(1, n_dp):
        sent = lax.dynamic_slice_in_dim(term, (me_dp ^ m) * columns, columns, axis=1)
        total = total + partner(sent, "dp", m)
    total = sum(exchange_rows(total, "tensor"))

    scan_grads, gate_grads = [None] * micro, [None] * micro
    column_parts = [[] for _ in range(n_dp)]
    for ts in ([0], list(range(1, micro))):
        held = jnp.concatenate([gathered[t] for t in ts], axis=0)
        for m in range(n_dp):
            block = lax.dynamic_slice_in_dim(held, (me_dp ^ m) * columns, columns, axis=1)
            column_parts[m].append(partner(block, "dp", m) if m else block)
        inner_rows = lax.dot_general(
            held, weight, (((1,), (1,)), ((), ())), preferred_element_type=F32
        )
        for i, t in enumerate(ts):
            mine_rows = inner_rows[i * group : (i + 1) * group].reshape(n, rows, inner)
            mine_rows = turned(mine_rows, (n - me) % n).reshape(group, inner)
            scan_grads[t] = (mine_rows * gate_f[t] * sig[t]).astype(BF16)
            gate_grads[t] = (
                mine_rows * scan_f[t] * sig[t] * (1.0 + gate_f[t] * (1.0 - sig[t]))
            ).astype(BF16)
    expert_grads = [
        (slot_prob[t] * jnp.dot(put[t], sources[t], preferred_element_type=F32)).astype(BF16)
        for t in range(micro)
    ]
    left = jnp.concatenate(gated_all, axis=0)
    right = jnp.concatenate([x for parts_m in column_parts for x in parts_m], axis=0)
    weight_grad = lax.dot_general(
        left, right, (((0,), (0,)), ((), ())), preferred_element_type=F32
    )
    return (
        passed_all[None],
        jnp.stack(scan_grads)[None],
        jnp.stack(gate_grads)[None],
        jnp.stack(expert_grads)[None],
        weight_grad[None],
        total[:experts].T[None],
        total[experts][None],
    )


def solution(mesh):
    placed = (
        P("section", None, ("dp", "tensor"), None),
        P("section", None, ("dp", "tensor"), None),
        P("section", None, ("dp", "tensor"), None, None),
        P("section", None, ("dp", "tensor"), None),
        P("section", None, ("dp", "tensor"), None),
        P("section", None, "dp", "tensor"),
        P("section", None, "dp", "tensor"),
        P("section", "tensor", None),
        P("section", "dp", None),
        P("section", "dp"),
    )
    return jax.shard_map(
        on_device,
        mesh=mesh,
        in_specs=placed,
        out_specs=(
            P("section", None, ("dp", "tensor"), None),
            P("section", None, "dp", "tensor"),
            P("section", None, "dp", "tensor"),
            P("section", None, ("dp", "tensor"), None),
            P("section", "tensor", "dp"),
            P("section", "dp", None),
            P("section", "dp"),
        ),
        check_vma=False,
    )
```

```python
import functools

import jax
import jax.numpy as jnp
from jax import lax
from jax.experimental import pallas as pl
from jax.experimental.pallas import tpu as pltpu
from jax.sharding import PartitionSpec as P

F32 = jnp.float32
BF16 = jnp.bfloat16
SMALL = pl.CostEstimate(flops=0, bytes_accessed=0, transcendentals=0)
PARAMS = pltpu.CompilerParams(vmem_limit_bytes=56 * 1024 * 1024)


def partner(shard, axis, mask):
    length = lax.axis_size(axis)
    return lax.ppermute(shard, axis, [(i, i ^ mask) for i in range(length)])


def around(shard, axis, by):
    length = lax.axis_size(axis)
    return lax.ppermute(shard, axis, [(i, (i + by) % length) for i in range(length)])


def exchange_rows(block):
    length = lax.axis_size("tensor")
    if length == 4:
        return [block] + [partner(block, "tensor", r) for r in range(1, length)]
    return [block] + [around(block, "tensor", length - r) for r in range(1, length)]


def first_stage(block):
    if lax.axis_size("tensor") != 4:
        return exchange_rows(block)
    return [block, partner(block, "tensor", 1), partner(block, "tensor", 2)]


def second_stage(held, *before):
    if lax.axis_size("tensor") != 4:
        return held
    block, one, two = lax.optimization_barrier(tuple(held) + before)[:3]
    middle = lax.ppermute(block, "tensor", [(1, 2), (2, 1)])
    ends = lax.ppermute(two, "tensor", [(2, 3), (1, 0)])
    return [block, one, two, middle, ends]


def joined(held, *before):
    if len(held) == lax.axis_size("tensor"):
        return held
    block, one, two, middle, ends = held
    middle, ends = lax.optimization_barrier((middle, ends) + before)[:2]
    me = lax.axis_index("tensor")
    inside = (me == 1) | (me == 2)
    return [block, one, two, jnp.where(inside, middle, ends)]


def position(r):
    n = lax.axis_size("tensor")
    me = lax.axis_index("tensor")
    return me ^ r if n == 4 else (me + r) % n


def tied(value, *others):
    return lax.optimization_barrier((value,) + others)[0]


def chunks(width):
    step = min(width, 1024)
    return [slice(i, i + step) for i in range(0, width, step)]


def selected(routes_ref, count):
    ids = routes_ref[...]
    column = lax.broadcasted_iota(jnp.int32, (ids.shape[0], count), 1)
    return [(ids[:, k : k + 1] == column).astype(F32) for k in range(ids.shape[1])]


def probs_kernel(experts, hidden_ref, small_ref, routes_ref, probs_ref, inv_ref, marked_ref):
    width = hidden_ref.shape[1]
    square = jnp.zeros((hidden_ref.shape[0], 1), F32)
    for c in chunks(width):
        h = hidden_ref[:, c].astype(F32)
        square += jnp.sum(h * h, axis=1, keepdims=True)
    inv = 1.0 / jnp.sqrt(square / width + 1e-05)
    logits = jnp.zeros((hidden_ref.shape[0], small_ref.shape[0]), F32)
    for c in chunks(width):
        gain = small_ref[experts : experts + 1, c].astype(F32)
        normed = (hidden_ref[:, c].astype(F32) * inv * gain).astype(BF16)
        logits += lax.dot_general(
            normed, small_ref[:, c], (((1,), (1,)), ((), ())), preferred_element_type=F32
        )
    column = lax.broadcasted_iota(jnp.int32, logits.shape, 1)
    weights = jnp.where(column < experts, jnp.exp(jnp.where(column < experts, logits, 0.0)), 0.0)
    probs = weights / jnp.sum(weights, axis=1, keepdims=True)
    probs_ref[...] = probs
    inv_ref[...] = inv
    named = sum(selected(routes_ref, logits.shape[1]))
    marked_ref[...] = jnp.where(named > 0, probs, -1.0)


def step_kernel(experts, parts, kept, choose, flag_ref, *refs):
    refs = list(refs)
    up_ref = refs.pop(0)
    other_ref = refs.pop(0) if choose else None
    hidden_ref, out_ref, routes_ref, probs_ref, inv_ref, small_ref = refs[:6]
    back_refs, refs = refs[6 : 6 + parts], refs[6 + parts :]
    passed_ref, term_ref, norm_ref, upstream_ref = refs
    width = up_ref.shape[2]
    rows = up_ref.shape[1]
    cap = back_refs[0].shape[1]
    t = pl.program_id(0)

    @pl.when(t == 0)
    def _():
        term_ref[...] = jnp.zeros_like(term_ref)

    choice = selected(routes_ref.at[0], probs_ref.shape[2])
    named = sum(choice)
    row = lax.broadcasted_iota(jnp.int32, (rows, rows), 0)
    column = lax.broadcasted_iota(jnp.int32, (rows, rows), 1)
    place = jnp.dot(
        (column < row).astype(BF16), named.astype(BF16), preferred_element_type=F32
    )
    expert = lax.broadcasted_iota(jnp.int32, named.shape, 1)
    slot = lax.broadcasted_iota(jnp.int32, (rows, cap), 1).astype(F32)
    picks = []
    for i in range(parts):
        mine = expert == flag_ref[1 + i]
        is_named = jnp.sum(jnp.where(mine, named, 0.0), axis=1, keepdims=True)
        at = jnp.sum(jnp.where(mine, place, 0.0), axis=1, keepdims=True)
        picks.append(jnp.where((at == slot) & (is_named > 0), 1.0, 0.0))
    pick = jnp.concatenate(picks, axis=1).astype(BF16)

    score = [jnp.zeros((rows, 1), F32) for _ in choice]
    for c in chunks(width):
        up = up_ref[0, :, c].astype(F32)
        if choose:
            up = jnp.where(flag_ref[0] == 1, up, other_ref[0, :, c].astype(F32))
        upstream_ref[:, c] = up
        for k in range(len(choice)):
            out = out_ref[0, :, k * width + c.start : k * width + c.stop].astype(F32)
            score[k] += jnp.sum(up * out, axis=1, keepdims=True)
    prob_grad = sum(a * b for a, b in zip(score, choice))
    p = probs_ref[0]
    logit_grad = (p * (prob_grad - jnp.sum(p * prob_grad, axis=1, keepdims=True))).astype(BF16)
    inv = inv_ref[0]
    mean = jnp.zeros((rows, 1), F32)
    for c in chunks(width):
        norm = jnp.dot(logit_grad, small_ref[:, c], preferred_element_type=F32)
        back = jnp.concatenate([ref[0, :, c] for ref in back_refs], axis=0)
        norm += jnp.dot(pick, back, preferred_element_type=F32)
        norm_ref[:, c] = norm
        gain = small_ref[experts : experts + 1, c].astype(F32)
        mean += jnp.sum(norm * gain * hidden_ref[0, :, c].astype(F32), axis=1, keepdims=True)
    mean = mean / width
    for c in chunks(width):
        gain = small_ref[experts : experts + 1, c].astype(F32)
        h = hidden_ref[0, :, c].astype(F32)
        grad = inv * (norm_ref[:, c] * gain) - h * inv**3 * mean
        passed_ref[0, :, c] = (upstream_ref[:, c] + grad).astype(BF16)

    @pl.when(t < kept)
    def _():
        for c in chunks(width):
            gain = small_ref[experts : experts + 1, c].astype(F32)
            scaled = hidden_ref[0, :, c].astype(F32) * inv
            normed = (scaled * gain).astype(BF16)
            router = lax.dot_general(
                logit_grad, normed, (((0,), (0,)), ((), ())), preferred_element_type=F32
            )
            gains = jnp.sum(norm_ref[:, c] * scaled, axis=0, keepdims=True)
            line = lax.broadcasted_iota(jnp.int32, router.shape, 0)
            term_ref[:, c] += jnp.where(line == experts, gains, router)


def gate_kernel(order_ref, scan_ref, gate_ref, out_ref):
    for r in range(out_ref.shape[1]):
        gate = gate_ref[0, order_ref[r]].astype(F32)
        scan = scan_ref[0, order_ref[r]].astype(F32)
        out_ref[0, r] = (scan * gate * (1.0 / (1.0 + jnp.exp(-gate)))).astype(BF16)


def inner_kernel(n, order_ref, *refs):
    blocks = refs[: 2 * n]
    weight_ref, scan_ref, gate_ref, scan_out, gate_out, held = refs[2 * n :]
    rows = blocks[0].shape[1]
    group = n * rows

    @pl.when(pl.program_id(0) == 0)
    def _():
        for i, ref in enumerate(blocks):
            for t in range(ref.shape[0]):
                step = t if i < n else t + 1
                start = pl.multiple_of(step * group + order_ref[i % n] * rows, 16)
                held[pl.ds(start, rows), :] = ref[t]

    inner = lax.dot_general(
        held[...], weight_ref[...], (((1,), (1,)), ((), ())), preferred_element_type=F32
    )
    for t in range(scan_ref.shape[0]):
        part = inner[t * group : (t + 1) * group]
        gate = gate_ref[t].astype(F32)
        scan = scan_ref[t].astype(F32)
        sig = 1.0 / (1.0 + jnp.exp(-gate))
        scan_out[t] = (part * gate * sig).astype(BF16)
        gate_out[t] = (part * scan * sig * (1.0 + gate * (1.0 - sig))).astype(BF16)


def columns_kernel(n, *refs):
    blocks, out_ref = refs[:n], refs[-1]
    rows = blocks[0].shape[1]
    for t in range(blocks[0].shape[0]):
        for r, ref in enumerate(blocks):
            start = (t * n + r) * rows
            out_ref[0, start : start + rows, :] = ref[t]
    if len(refs) > n + 1:
        start = blocks[0].shape[0] * n * rows
        out_ref[0, start:, :] = (refs[n][...] + refs[n + 1][...]).astype(BF16)


def weight_kernel(order_ref, *refs):
    lefts, (first_ref, later_ref, out_ref, held) = refs[:-4], refs[-4:]
    groups, rows, _ = first_ref.shape
    depth = lefts[0].shape[0]

    @pl.when(pl.program_id(0) == 0)
    def _():
        for g in range(groups):
            start = pl.multiple_of(order_ref[g] * depth, 16)
            held[pl.ds(start, rows), :] = first_ref[g]
            start = pl.multiple_of(order_ref[g] * depth + rows, 16)
            held[pl.ds(start, depth - rows), :] = later_ref[g, : depth - rows, :]

    left = jnp.concatenate([ref[...] for ref in lefts], axis=0)
    out_ref[...] = lax.dot_general(
        left, held[...], (((0,), (0,)), ((), ())), preferred_element_type=F32
    )


def dispatch_kernel(n, order_ref, marks_ref, *refs):
    out_ref = refs[2 * n]
    _, rows, width = refs[0].shape
    cap = out_ref.shape[1] // n
    row = lax.broadcasted_iota(jnp.int32, (rows, rows), 0)
    column = lax.broadcasted_iota(jnp.int32, (rows, rows), 1)
    before = (row < column).astype(BF16)
    slot = lax.broadcasted_iota(jnp.int32, (cap, rows), 0).astype(F32)
    owner = lax.broadcasted_iota(jnp.int32, (n * cap, rows), 0) // cap
    puts, prob = [], 0.0
    for r in range(n):
        mark = marks_ref[0, r : r + 1, :]
        named = (mark >= 0).astype(F32)
        place = jnp.dot(named.astype(BF16), before, preferred_element_type=F32)
        put = jnp.where((slot == place) & (named > 0), 1.0, 0.0)
        put = jnp.where(owner == order_ref[r], jnp.concatenate([put] * n, axis=0), 0.0)
        prob += jnp.sum(put * mark, axis=1, keepdims=True)
        puts.append(put)
    put = jnp.concatenate(puts, axis=1).astype(BF16)

    def fill(sources):
        for c in chunks(width):
            source = jnp.concatenate([ref[0, :, c] for ref in sources], axis=0)
            moved = jnp.dot(put, source, preferred_element_type=F32)
            out_ref[0, :, c] = (prob * moved).astype(BF16)

    @pl.when(pl.program_id(0) == 0)
    def _():
        fill(refs[:n])

    @pl.when(pl.program_id(0) > 0)
    def _():
        fill(refs[n : 2 * n])


def whole_spec(array, extra=0):
    zeros = (0,) * array.ndim
    return pl.BlockSpec(array.shape, lambda *_: zeros, pipeline_mode=pl.Buffered(1))


def on_device(
    incoming, hidden, expert_out, routes, expert_back, scan_out, gate_in, w_out, w_router, norm_gain
):
    micro = incoming.shape[1]
    rows = incoming.shape[2]
    width = incoming.shape[3]
    experts = w_router.shape[2]
    n = lax.axis_size("tensor")
    n_dp = lax.axis_size("dp")
    cap = expert_back.shape[2] // n
    inner = scan_out.shape[3]
    group = scan_out.shape[2]
    columns = width // n_dp
    padded = -(-(experts + 1) // 16) * 16
    me = lax.axis_index("tensor")
    me_dp = lax.axis_index("dp")
    section = lax.axis_index("section")
    upper = section == 1
    order = jnp.stack([position(r) for r in range(n)]).astype(jnp.int32)
    weight = w_out[0]
    call = functools.partial(pl.pallas_call, compiler_params=PARAMS, cost_estimate=SMALL)

    back = expert_back[0].reshape(micro, n, cap, width)
    returned = [lax.dynamic_index_in_dim(back, me, 1, False)]
    for r in range(1, n):
        if n == 4:
            block = lax.dynamic_index_in_dim(back, me ^ r, 1, False)
            returned.append(partner(block, "tensor", r))
        else:
            block = lax.dynamic_index_in_dim(back, (me + n - r) % n, 1, False)
            returned.append(around(block, "tensor", n - r))

    small = jnp.concatenate([w_router[0].T, norm_gain[0][None]], axis=0)
    smalls = lax.all_gather(small, "dp", axis=1, tiled=True)
    smalls = jnp.pad(smalls, ((0, padded - experts - 1), (0, 0)))

    probs, inv_rms, marked = call(
        functools.partial(probs_kernel, experts),
        out_shape=(
            jax.ShapeDtypeStruct((micro * rows, padded), F32),
            jax.ShapeDtypeStruct((micro * rows, 1), F32),
            jax.ShapeDtypeStruct((micro * rows, padded), F32),
        ),
        name="probs",
    )(hidden[0].reshape(micro * rows, width), smalls, routes[0].reshape(micro * rows, -1))
    probs = probs.reshape(micro, rows, padded)
    inv_rms = inv_rms.reshape(micro, rows, 1)
    out_rows = expert_out[0].reshape(micro, rows, -1)
    flag = jnp.concatenate([section.astype(jnp.int32)[None], order])

    def step_back(t0, t1, kept, upstream, other=None):
        count = t1 - t0
        shifted = [hidden[0], out_rows, routes[0], probs, inv_rms]
        arrays, shift = [upstream], [t0]
        if other is not None:
            arrays, shift = arrays + [other], shift + [0]
        arrays, shift = arrays + shifted, shift + [t0] * len(shifted)
        specs = []
        for a, s in zip(arrays, shift):
            rest = (0,) * (a.ndim - 1)
            specs.append(
                pl.BlockSpec((1,) + a.shape[1:], lambda t, s=s, rest=rest: (t + s,) + rest)
            )
        arrays.append(smalls)
        specs.append(whole_spec(smalls))
        for a in returned:
            specs.append(pl.BlockSpec((1,) + a.shape[1:], lambda t: (t + t0, 0, 0)))
            arrays.append(a)
        return call(
            functools.partial(step_kernel, experts, len(returned), kept, other is not None),
            grid=(count,),
            out_shape=(
                jax.ShapeDtypeStruct((count, rows, width), BF16),
                jax.ShapeDtypeStruct((padded, width), F32),
            ),
            in_specs=[pl.BlockSpec(memory_space=pltpu.SMEM)] + specs,
            out_specs=(
                pl.BlockSpec((1, rows, width), lambda t: (t, 0, 0)),
                pl.BlockSpec((padded, width), lambda t: (0, 0)),
            ),
            scratch_shapes=[pltpu.VMEM((rows, width), F32)] * 2,
            name="step",
        )(flag, *arrays)

    def columns_over(blocks, terms=()):
        count = blocks[0].shape[0]
        high = count * group + (padded if terms else 0)
        split = call(
            functools.partial(columns_kernel, n),
            grid=(n_dp,),
            out_shape=jax.ShapeDtypeStruct((n_dp, high, columns), BF16),
            in_specs=[pl.BlockSpec((count, rows, columns), lambda g: (0, 0, g))] * n
            + [pl.BlockSpec((padded, columns), lambda g: (0, g))] * len(terms),
            out_specs=pl.BlockSpec((1, high, columns), lambda g: (g, 0, 0)),
            name="columns",
        )(*blocks, *terms)
        return lax.all_to_all(split, "dp", split_axis=0, concat_axis=0, tiled=True)

    first, term_first = step_back(0, micro - 1, 1, incoming[0])
    received = lax.ppermute(first, "section", [(1, 0)])
    near_rows = exchange_rows(first[:1])

    four = (micro, n, rows, inner)
    spec = pl.BlockSpec((1, n, rows, inner), lambda t, o: (t, 0, 0, 0))
    gated = call(
        gate_kernel,
        out_shape=jax.ShapeDtypeStruct(four, BF16),
        grid_spec=pltpu.PrefetchScalarGridSpec(
            num_scalar_prefetch=1, grid=(micro,), in_specs=[spec] * 2, out_specs=spec
        ),
        name="gate",
    )(order, tied(scan_out[0].reshape(four), first), gate_in[0].reshape(four))
    gated = gated.reshape(micro * group, inner)
    if n_dp == 4:
        across = partner(gated, "dp", 2)
        lefts = [gated, partner(gated, "dp", 1), across, partner(across, "dp", 1)]
    else:
        lefts = [gated] + [partner(gated, "dp", m) for m in range(1, n_dp)]


    later, term_later = step_back(
        1, micro, micro, incoming[0], received
    )
    passed_all = jnp.concatenate([first[:1], later], axis=0)
    far_half = first_stage(tied(later, *near_rows[1:]))
    far_rows = joined(second_stage(far_half, *lefts))
    across_first = columns_over([tied(near_rows[0], *far_half[1:])] + near_rows[1:])
    upstream = jnp.where(upper, incoming[0, 1:], received)
    source_first = joined(second_stage(first_stage(tied(incoming[0, :1], *far_half[1:]))))
    source_half = first_stage(tied(upstream, *source_first[1:]))
    rights = [across_first, columns_over(
        [tied(far_rows[0], across_first)] + far_rows[1:], (term_first, term_later)
    )]

    tile = min(inner, 256)
    blocks = near_rows + far_rows
    rows_spec = pl.BlockSpec((micro, group, tile), lambda i, o: (0, 0, i))
    scan_grad, gate_grad = call(
        functools.partial(inner_kernel, n),
        out_shape=[jax.ShapeDtypeStruct((micro, group, inner), BF16)] * 2,
        grid_spec=pltpu.PrefetchScalarGridSpec(
            num_scalar_prefetch=1,
            grid=(inner // tile,),
            in_specs=[whole_spec(b) for b in blocks]
            + [pl.BlockSpec((tile, width), lambda i, o: (i, 0))]
            + [rows_spec] * 2,
            out_specs=[rows_spec] * 2,
            scratch_shapes=[pltpu.VMEM((micro * group, width), BF16)],
        ),
        name="project",
    )(order, *blocks, weight, scan_out[0], gate_in[0])

    source_later = second_stage(source_half, scan_grad)
    depth = lefts[0].shape[0]
    order_dp = me_dp ^ jnp.arange(n_dp, dtype=jnp.int32)
    weight_grad = call(
        weight_kernel,
        out_shape=jax.ShapeDtypeStruct((inner, columns), F32),
        grid_spec=pltpu.PrefetchScalarGridSpec(
            num_scalar_prefetch=1,
            grid=(inner // tile,),
            in_specs=[pl.BlockSpec((depth, tile), lambda i, o: (0, i))] * n_dp
            + [whole_spec(x) for x in rights],
            out_specs=pl.BlockSpec((tile, columns), lambda i, o: (i, 0)),
            scratch_shapes=[pltpu.VMEM((n_dp * depth, columns), BF16)],
        ),
        name="weight_grad",
    )(order_dp, *lefts, *rights)

    source_later = joined(source_later, weight_grad)
    total = jnp.sum(tied(rights[1], scan_grad)[:, -padded:].astype(F32), axis=0)[: experts + 1]
    marks = marked[:, :experts].T.reshape(1, -1)
    marks = jnp.pad(marks, ((0, 0), (0, -marks.shape[1] % columns))).reshape(-1, columns)
    if n == 4:
        both = partner(jnp.concatenate([total, marks], axis=0), "tensor", 1)
        total = total + both[: experts + 1]
        marks = jnp.concatenate([marks, both[experts + 1 :]], axis=0)
        both = partner(jnp.concatenate([total, marks], axis=0), "tensor", 2)
        total = total + both[: experts + 1]
        marks = jnp.concatenate([marks, both[experts + 1 :]], axis=0)
    else:
        shared = exchange_rows(jnp.concatenate([total, marks], axis=0))
        total = sum(x[: experts + 1] for x in shared)
        marks = jnp.concatenate([x[experts + 1 :] for x in shared], axis=0)
    marks = marks.reshape(n, -1)[:, : experts * micro * rows].reshape(n, experts, micro, rows)
    mine = jnp.swapaxes(lax.dynamic_index_in_dim(marks, me, 1, False), 0, 1)

    expert_grad = call(
        functools.partial(dispatch_kernel, n),
        out_shape=jax.ShapeDtypeStruct((micro, n * cap, width), BF16),
        grid_spec=pltpu.PrefetchScalarGridSpec(
            num_scalar_prefetch=1,
            grid=(micro,),
            in_specs=[pl.BlockSpec((1, n, rows), lambda t, o: (t, 0, 0))]
            + [whole_spec(x) for x in source_first]
            + [pl.BlockSpec((1, rows, width), lambda t, o: (jnp.maximum(t - 1, 0), 0, 0))] * n,
            out_specs=pl.BlockSpec((1, n * cap, width), lambda t, o: (t, 0, 0)),
        ),
        name="dispatch",
    )(order, mine, *source_first, *source_later)

    return (
        passed_all[None],
        scan_grad[None],
        gate_grad[None],
        expert_grad[None],
        weight_grad[None],
        total[:experts].T[None],
        total[experts][None],
    )


def solution(mesh):
    placed = (
        P("section", None, ("dp", "tensor"), None),
        P("section", None, ("dp", "tensor"), None),
        P("section", None, ("dp", "tensor"), None, None),
        P("section", None, ("dp", "tensor"), None),
        P("section", None, ("dp", "tensor"), None),
        P("section", None, "dp", "tensor"),
        P("section", None, "dp", "tensor"),
        P("section", "tensor", None),
        P("section", "dp", None),
        P("section", "dp"),
    )
    return jax.shard_map(
        on_device,
        mesh=mesh,
        in_specs=placed,
        out_specs=(
            P("section", None, ("dp", "tensor"), None),
            P("section", None, "dp", "tensor"),
            P("section", None, "dp", "tensor"),
            P("section", None, ("dp", "tensor"), None),
            P("section", "tensor", "dp"),
            P("section", "dp", None),
            P("section", "dp"),
        ),
        check_vma=False,
    )
```

```python
import functools

import jax
import jax.numpy as jnp
from jax import lax
from jax.experimental import pallas as pl
from jax.experimental.pallas import tpu as pltpu
from jax.sharding import PartitionSpec as P

F32 = jnp.float32
BF16 = jnp.bfloat16
SMALL = pl.CostEstimate(flops=0, bytes_accessed=0, transcendentals=0)
PARAMS = pltpu.CompilerParams(vmem_limit_bytes=56 * 1024 * 1024)


def partner(shard, axis, mask):
    length = lax.axis_size(axis)
    return lax.ppermute(shard, axis, [(i, i ^ mask) for i in range(length)])


def around(shard, axis, by):
    length = lax.axis_size(axis)
    return lax.ppermute(shard, axis, [(i, (i + by) % length) for i in range(length)])


def exchange_rows(block):
    length = lax.axis_size("tensor")
    if length == 4:
        return [block] + [partner(block, "tensor", r) for r in range(1, length)]
    return [block] + [around(block, "tensor", length - r) for r in range(1, length)]


def first_stage(block):
    if lax.axis_size("tensor") != 4:
        return exchange_rows(block)
    return [block, partner(block, "tensor", 1), partner(block, "tensor", 2)]


def second_stage(held, *before):
    if lax.axis_size("tensor") != 4:
        return held
    block, one, two = lax.optimization_barrier(tuple(held) + before)[:3]
    middle = lax.ppermute(block, "tensor", [(1, 2), (2, 1)])
    ends = lax.ppermute(two, "tensor", [(2, 3), (1, 0)])
    return [block, one, two, middle, ends]


def joined(held, *before):
    if len(held) == lax.axis_size("tensor"):
        return held
    block, one, two, middle, ends = held
    middle, ends = lax.optimization_barrier((middle, ends) + before)[:2]
    me = lax.axis_index("tensor")
    inside = (me == 1) | (me == 2)
    return [block, one, two, jnp.where(inside, middle, ends)]


def position(r):
    n = lax.axis_size("tensor")
    me = lax.axis_index("tensor")
    return me ^ r if n == 4 else (me + r) % n


def tied(value, *others):
    return lax.optimization_barrier((value,) + others)[0]


def chunks(width):
    step = min(width, 1024)
    return [slice(i, i + step) for i in range(0, width, step)]


def selected(routes_ref, count):
    ids = routes_ref[...]
    column = lax.broadcasted_iota(jnp.int32, (ids.shape[0], count), 1)
    return [(ids[:, k : k + 1] == column).astype(F32) for k in range(ids.shape[1])]


def probs_kernel(experts, hidden_ref, small_ref, routes_ref, probs_ref, inv_ref, marked_ref):
    width = hidden_ref.shape[1]
    square = jnp.zeros((hidden_ref.shape[0], 1), F32)
    for c in chunks(width):
        h = hidden_ref[:, c].astype(F32)
        square += jnp.sum(h * h, axis=1, keepdims=True)
    inv = 1.0 / jnp.sqrt(square / width + 1e-05)
    logits = jnp.zeros((hidden_ref.shape[0], small_ref.shape[0]), F32)
    for c in chunks(width):
        gain = small_ref[experts : experts + 1, c].astype(F32)
        normed = (hidden_ref[:, c].astype(F32) * inv * gain).astype(BF16)
        logits += lax.dot_general(
            normed, small_ref[:, c], (((1,), (1,)), ((), ())), preferred_element_type=F32
        )
    column = lax.broadcasted_iota(jnp.int32, logits.shape, 1)
    weights = jnp.where(column < experts, jnp.exp(jnp.where(column < experts, logits, 0.0)), 0.0)
    probs = weights / jnp.sum(weights, axis=1, keepdims=True)
    probs_ref[...] = probs
    inv_ref[...] = inv
    named = sum(selected(routes_ref, logits.shape[1]))
    marked_ref[...] = jnp.where(named > 0, probs, -1.0)


def step_kernel(experts, parts, kept, choose, flag_ref, *refs):
    refs = list(refs)
    up_ref = refs.pop(0)
    other_ref = refs.pop(0) if choose else None
    hidden_ref, out_ref, routes_ref, probs_ref, inv_ref, small_ref = refs[:6]
    back_refs, refs = refs[6 : 6 + parts], refs[6 + parts :]
    passed_ref, term_ref, norm_ref, upstream_ref = refs
    width = up_ref.shape[2]
    rows = up_ref.shape[1]
    cap = back_refs[0].shape[1]
    t = pl.program_id(0)

    @pl.when(t == 0)
    def _():
        term_ref[...] = jnp.zeros_like(term_ref)

    choice = selected(routes_ref.at[0], probs_ref.shape[2])
    named = sum(choice)
    row = lax.broadcasted_iota(jnp.int32, (rows, rows), 0)
    column = lax.broadcasted_iota(jnp.int32, (rows, rows), 1)
    place = jnp.dot(
        (column < row).astype(BF16), named.astype(BF16), preferred_element_type=F32
    )
    expert = lax.broadcasted_iota(jnp.int32, named.shape, 1)
    slot = lax.broadcasted_iota(jnp.int32, (rows, cap), 1).astype(F32)
    picks = []
    for i in range(parts):
        mine = expert == flag_ref[1 + i]
        is_named = jnp.sum(jnp.where(mine, named, 0.0), axis=1, keepdims=True)
        at = jnp.sum(jnp.where(mine, place, 0.0), axis=1, keepdims=True)
        picks.append(jnp.where((at == slot) & (is_named > 0), 1.0, 0.0))
    pick = jnp.concatenate(picks, axis=1).astype(BF16)

    score = [jnp.zeros((rows, 1), F32) for _ in choice]
    for c in chunks(width):
        up = up_ref[0, :, c].astype(F32)
        if choose:
            up = jnp.where(flag_ref[0] == 1, up, other_ref[0, :, c].astype(F32))
        upstream_ref[:, c] = up
        for k in range(len(choice)):
            out = out_ref[0, :, k * width + c.start : k * width + c.stop].astype(F32)
            score[k] += jnp.sum(up * out, axis=1, keepdims=True)
    prob_grad = sum(a * b for a, b in zip(score, choice))
    p = probs_ref[0]
    logit_grad = (p * (prob_grad - jnp.sum(p * prob_grad, axis=1, keepdims=True))).astype(BF16)
    inv = inv_ref[0]
    mean = jnp.zeros((rows, 1), F32)
    for c in chunks(width):
        norm = jnp.dot(logit_grad, small_ref[:, c], preferred_element_type=F32)
        back = jnp.concatenate([ref[0, :, c] for ref in back_refs], axis=0)
        norm += jnp.dot(pick, back, preferred_element_type=F32)
        norm_ref[:, c] = norm
        gain = small_ref[experts : experts + 1, c].astype(F32)
        mean += jnp.sum(norm * gain * hidden_ref[0, :, c].astype(F32), axis=1, keepdims=True)
    mean = mean / width
    for c in chunks(width):
        gain = small_ref[experts : experts + 1, c].astype(F32)
        h = hidden_ref[0, :, c].astype(F32)
        grad = inv * (norm_ref[:, c] * gain) - h * inv**3 * mean
        passed_ref[0, :, c] = (upstream_ref[:, c] + grad).astype(BF16)

    @pl.when(t < kept)
    def _():
        for c in chunks(width):
            gain = small_ref[experts : experts + 1, c].astype(F32)
            scaled = hidden_ref[0, :, c].astype(F32) * inv
            normed = (scaled * gain).astype(BF16)
            router = lax.dot_general(
                logit_grad, normed, (((0,), (0,)), ((), ())), preferred_element_type=F32
            )
            gains = jnp.sum(norm_ref[:, c] * scaled, axis=0, keepdims=True)
            line = lax.broadcasted_iota(jnp.int32, router.shape, 0)
            term_ref[:, c] += jnp.where(line == experts, gains, router)


def gate_kernel(order_ref, scan_ref, gate_ref, out_ref):
    for r in range(out_ref.shape[1]):
        gate = gate_ref[0, order_ref[r]].astype(F32)
        scan = scan_ref[0, order_ref[r]].astype(F32)
        out_ref[0, r] = (scan * gate * (1.0 / (1.0 + jnp.exp(-gate)))).astype(BF16)


def inner_kernel(n, order_ref, *refs):
    blocks = refs[: 2 * n]
    weight_ref, scan_ref, gate_ref, scan_out, gate_out, held = refs[2 * n :]
    rows = blocks[0].shape[1]
    group = n * rows

    @pl.when(pl.program_id(0) == 0)
    def _():
        for i, ref in enumerate(blocks):
            for t in range(ref.shape[0]):
                step = t if i < n else t + 1
                start = pl.multiple_of(step * group + order_ref[i % n] * rows, 16)
                held[pl.ds(start, rows), :] = ref[t]

    inner = lax.dot_general(
        held[...], weight_ref[...], (((1,), (1,)), ((), ())), preferred_element_type=F32
    )
    for t in range(scan_ref.shape[0]):
        part = inner[t * group : (t + 1) * group]
        gate = gate_ref[t].astype(F32)
        scan = scan_ref[t].astype(F32)
        sig = 1.0 / (1.0 + jnp.exp(-gate))
        scan_out[t] = (part * gate * sig).astype(BF16)
        gate_out[t] = (part * scan * sig * (1.0 + gate * (1.0 - sig))).astype(BF16)


def columns_kernel(n, *refs):
    blocks, out_ref = refs[:n], refs[-1]
    rows = blocks[0].shape[1]
    for t in range(blocks[0].shape[0]):
        for r, ref in enumerate(blocks):
            start = (t * n + r) * rows
            out_ref[0, start : start + rows, :] = ref[t]
    if len(refs) > n + 1:
        start = blocks[0].shape[0] * n * rows
        out_ref[0, start:, :] = (refs[n][...] + refs[n + 1][...]).astype(BF16)


def weight_kernel(order_ref, *refs):
    lefts, (first_ref, later_ref, out_ref, held) = refs[:-4], refs[-4:]
    groups, rows, _ = first_ref.shape
    depth = lefts[0].shape[0]

    @pl.when(pl.program_id(0) == 0)
    def _():
        for g in range(groups):
            start = pl.multiple_of(order_ref[g] * depth, 16)
            held[pl.ds(start, rows), :] = first_ref[g]
            start = pl.multiple_of(order_ref[g] * depth + rows, 16)
            held[pl.ds(start, depth - rows), :] = later_ref[g, : depth - rows, :]

    left = jnp.concatenate([ref[...] for ref in lefts], axis=0)
    out_ref[...] = lax.dot_general(
        left, held[...], (((0,), (0,)), ((), ())), preferred_element_type=F32
    )


def dispatch_kernel(n, order_ref, marks_ref, *refs):
    out_ref = refs[2 * n]
    _, rows, width = refs[0].shape
    cap = out_ref.shape[1] // n
    row = lax.broadcasted_iota(jnp.int32, (rows, rows), 0)
    column = lax.broadcasted_iota(jnp.int32, (rows, rows), 1)
    before = (row < column).astype(BF16)
    slot = lax.broadcasted_iota(jnp.int32, (cap, rows), 0).astype(F32)
    owner = lax.broadcasted_iota(jnp.int32, (n * cap, rows), 0) // cap
    puts, prob = [], 0.0
    for r in range(n):
        mark = marks_ref[0, r : r + 1, :]
        named = (mark >= 0).astype(F32)
        place = jnp.dot(named.astype(BF16), before, preferred_element_type=F32)
        put = jnp.where((slot == place) & (named > 0), 1.0, 0.0)
        put = jnp.where(owner == order_ref[r], jnp.concatenate([put] * n, axis=0), 0.0)
        prob += jnp.sum(put * mark, axis=1, keepdims=True)
        puts.append(put)
    put = jnp.concatenate(puts, axis=1).astype(BF16)

    def fill(sources):
        for c in chunks(width):
            source = jnp.concatenate([ref[0, :, c] for ref in sources], axis=0)
            moved = jnp.dot(put, source, preferred_element_type=F32)
            out_ref[0, :, c] = (prob * moved).astype(BF16)

    @pl.when(pl.program_id(0) == 0)
    def _():
        fill(refs[:n])

    @pl.when(pl.program_id(0) > 0)
    def _():
        fill(refs[n : 2 * n])


def whole_spec(array, extra=0):
    zeros = (0,) * array.ndim
    return pl.BlockSpec(array.shape, lambda *_: zeros, pipeline_mode=pl.Buffered(1))


def on_device(
    incoming, hidden, expert_out, routes, expert_back, scan_out, gate_in, w_out, w_router, norm_gain
):
    micro = incoming.shape[1]
    rows = incoming.shape[2]
    width = incoming.shape[3]
    experts = w_router.shape[2]
    n = lax.axis_size("tensor")
    n_dp = lax.axis_size("dp")
    cap = expert_back.shape[2] // n
    inner = scan_out.shape[3]
    group = scan_out.shape[2]
    columns = width // n_dp
    padded = -(-(experts + 1) // 16) * 16
    me = lax.axis_index("tensor")
    me_dp = lax.axis_index("dp")
    section = lax.axis_index("section")
    upper = section == 1
    order = jnp.stack([position(r) for r in range(n)]).astype(jnp.int32)
    weight = w_out[0]
    call = functools.partial(pl.pallas_call, compiler_params=PARAMS, cost_estimate=SMALL)

    back = expert_back[0].reshape(micro, n, cap, width)
    returned = [lax.dynamic_index_in_dim(back, me, 1, False)]
    for r in range(1, n):
        if n == 4:
            block = lax.dynamic_index_in_dim(back, me ^ r, 1, False)
            returned.append(partner(block, "tensor", r))
        else:
            block = lax.dynamic_index_in_dim(back, (me + n - r) % n, 1, False)
            returned.append(around(block, "tensor", n - r))

    small = jnp.concatenate([w_router[0].T, norm_gain[0][None]], axis=0)
    smalls = lax.all_gather(small, "dp", axis=1, tiled=True)
    smalls = jnp.pad(smalls, ((0, padded - experts - 1), (0, 0)))

    probs, inv_rms, marked = call(
        functools.partial(probs_kernel, experts),
        out_shape=(
            jax.ShapeDtypeStruct((micro * rows, padded), F32),
            jax.ShapeDtypeStruct((micro * rows, 1), F32),
            jax.ShapeDtypeStruct((micro * rows, padded), F32),
        ),
        name="probs",
    )(hidden[0].reshape(micro * rows, width), smalls, routes[0].reshape(micro * rows, -1))
    probs = probs.reshape(micro, rows, padded)
    inv_rms = inv_rms.reshape(micro, rows, 1)
    out_rows = expert_out[0].reshape(micro, rows, -1)
    flag = jnp.concatenate([section.astype(jnp.int32)[None], order])

    def step_back(t0, t1, kept, upstream, other=None):
        count = t1 - t0
        shifted = [hidden[0], out_rows, routes[0], probs, inv_rms]
        arrays, shift = [upstream], [t0]
        if other is not None:
            arrays, shift = arrays + [other], shift + [0]
        arrays, shift = arrays + shifted, shift + [t0] * len(shifted)
        specs = []
        for a, s in zip(arrays, shift):
            rest = (0,) * (a.ndim - 1)
            specs.append(
                pl.BlockSpec((1,) + a.shape[1:], lambda t, s=s, rest=rest: (t + s,) + rest)
            )
        arrays.append(smalls)
        specs.append(whole_spec(smalls))
        for a in returned:
            specs.append(pl.BlockSpec((1,) + a.shape[1:], lambda t: (t + t0, 0, 0)))
            arrays.append(a)
        return call(
            functools.partial(step_kernel, experts, len(returned), kept, other is not None),
            grid=(count,),
            out_shape=(
                jax.ShapeDtypeStruct((count, rows, width), BF16),
                jax.ShapeDtypeStruct((padded, width), F32),
            ),
            in_specs=[pl.BlockSpec(memory_space=pltpu.SMEM)] + specs,
            out_specs=(
                pl.BlockSpec((1, rows, width), lambda t: (t, 0, 0)),
                pl.BlockSpec((padded, width), lambda t: (0, 0)),
            ),
            scratch_shapes=[pltpu.VMEM((rows, width), F32)] * 2,
            name="step",
        )(flag, *arrays)

    four = (micro, n, rows, inner)
    spec = pl.BlockSpec((1, n, rows, inner), lambda t, o: (t, 0, 0, 0))
    gated = call(
        gate_kernel,
        out_shape=jax.ShapeDtypeStruct(four, BF16),
        grid_spec=pltpu.PrefetchScalarGridSpec(
            num_scalar_prefetch=1, grid=(micro,), in_specs=[spec] * 2, out_specs=spec
        ),
        name="gate",
    )(order, tied(scan_out[0].reshape(four), probs), gate_in[0].reshape(four))

    def columns_over(blocks, terms=()):
        count = blocks[0].shape[0]
        high = count * group + (padded if terms else 0)
        split = call(
            functools.partial(columns_kernel, n),
            grid=(n_dp,),
            out_shape=jax.ShapeDtypeStruct((n_dp, high, columns), BF16),
            in_specs=[pl.BlockSpec((count, rows, columns), lambda g: (0, 0, g))] * n
            + [pl.BlockSpec((padded, columns), lambda g: (0, g))] * len(terms),
            out_specs=pl.BlockSpec((1, high, columns), lambda g: (g, 0, 0)),
            name="columns",
        )(*blocks, *terms)
        return lax.all_to_all(split, "dp", split_axis=0, concat_axis=0, tiled=True)

    first, term_first = step_back(0, micro - 1, 1, tied(incoming[0], gated))
    received = lax.ppermute(first, "section", [(1, 0)])
    near_rows = exchange_rows(first[:1])

    gated = tied(gated.reshape(micro * group, inner), first)
    if n_dp == 4:
        across = partner(gated, "dp", 2)
        lefts = [gated, partner(gated, "dp", 1), across, partner(across, "dp", 1)]
    else:
        lefts = [gated] + [partner(gated, "dp", m) for m in range(1, n_dp)]


    later, term_later = step_back(
        1, micro, micro, incoming[0], received
    )
    passed_all = jnp.concatenate([first[:1], later], axis=0)
    far_half = first_stage(tied(later, *near_rows[1:]))
    far_rows = joined(second_stage(far_half, *lefts))
    across_first = columns_over([tied(near_rows[0], *far_half[1:])] + near_rows[1:])
    upstream = jnp.where(upper, incoming[0, 1:], received)
    source_first = joined(second_stage(first_stage(tied(incoming[0, :1], *far_half[1:]))))
    source_half = first_stage(tied(upstream, *source_first[1:]))
    rights = [across_first, columns_over(
        [tied(far_rows[0], across_first)] + far_rows[1:], (term_first, term_later)
    )]

    tile = min(inner, 256)
    blocks = near_rows + far_rows
    rows_spec = pl.BlockSpec((micro, group, tile), lambda i, o: (0, 0, i))
    scan_grad, gate_grad = call(
        functools.partial(inner_kernel, n),
        out_shape=[jax.ShapeDtypeStruct((micro, group, inner), BF16)] * 2,
        grid_spec=pltpu.PrefetchScalarGridSpec(
            num_scalar_prefetch=1,
            grid=(inner // tile,),
            in_specs=[whole_spec(b) for b in blocks]
            + [pl.BlockSpec((tile, width), lambda i, o: (i, 0))]
            + [rows_spec] * 2,
            out_specs=[rows_spec] * 2,
            scratch_shapes=[pltpu.VMEM((micro * group, width), BF16)],
        ),
        name="project",
    )(order, *blocks, weight, scan_out[0], gate_in[0])

    source_later = second_stage(source_half, scan_grad)
    depth = lefts[0].shape[0]
    order_dp = me_dp ^ jnp.arange(n_dp, dtype=jnp.int32)
    weight_grad = call(
        weight_kernel,
        out_shape=jax.ShapeDtypeStruct((inner, columns), F32),
        grid_spec=pltpu.PrefetchScalarGridSpec(
            num_scalar_prefetch=1,
            grid=(inner // tile,),
            in_specs=[pl.BlockSpec((depth, tile), lambda i, o: (0, i))] * n_dp
            + [whole_spec(x) for x in rights],
            out_specs=pl.BlockSpec((tile, columns), lambda i, o: (i, 0)),
            scratch_shapes=[pltpu.VMEM((n_dp * depth, columns), BF16)],
        ),
        name="weight_grad",
    )(order_dp, *lefts, *rights)

    source_later = joined(source_later, weight_grad)
    total = jnp.sum(tied(rights[1], scan_grad)[:, -padded:].astype(F32), axis=0)[: experts + 1]
    marks = marked[:, :experts].T.reshape(1, -1)
    marks = jnp.pad(marks, ((0, 0), (0, -marks.shape[1] % columns))).reshape(-1, columns)
    shared = exchange_rows(jnp.concatenate([total, marks], axis=0))
    total = sum(x[: experts + 1] for x in shared)
    marks = jnp.concatenate([x[experts + 1 :] for x in shared], axis=0)
    marks = marks.reshape(n, -1)[:, : experts * micro * rows].reshape(n, experts, micro, rows)
    mine = jnp.swapaxes(lax.dynamic_index_in_dim(marks, me, 1, False), 0, 1)

    expert_grad = call(
        functools.partial(dispatch_kernel, n),
        out_shape=jax.ShapeDtypeStruct((micro, n * cap, width), BF16),
        grid_spec=pltpu.PrefetchScalarGridSpec(
            num_scalar_prefetch=1,
            grid=(micro,),
            in_specs=[pl.BlockSpec((1, n, rows), lambda t, o: (t, 0, 0))]
            + [whole_spec(x) for x in source_first]
            + [pl.BlockSpec((1, rows, width), lambda t, o: (jnp.maximum(t - 1, 0), 0, 0))] * n,
            out_specs=pl.BlockSpec((1, n * cap, width), lambda t, o: (t, 0, 0)),
        ),
        name="dispatch",
    )(order, mine, *source_first, *source_later)

    return (
        passed_all[None],
        scan_grad[None],
        gate_grad[None],
        expert_grad[None],
        weight_grad[None],
        total[:experts].T[None],
        total[experts][None],
    )


def solution(mesh):
    placed = (
        P("section", None, ("dp", "tensor"), None),
        P("section", None, ("dp", "tensor"), None),
        P("section", None, ("dp", "tensor"), None, None),
        P("section", None, ("dp", "tensor"), None),
        P("section", None, ("dp", "tensor"), None),
        P("section", None, "dp", "tensor"),
        P("section", None, "dp", "tensor"),
        P("section", "tensor", None),
        P("section", "dp", None),
        P("section", "dp"),
    )
    return jax.shard_map(
        on_device,
        mesh=mesh,
        in_specs=placed,
        out_specs=(
            P("section", None, ("dp", "tensor"), None),
            P("section", None, "dp", "tensor"),
            P("section", None, "dp", "tensor"),
            P("section", None, ("dp", "tensor"), None),
            P("section", "tensor", "dp"),
            P("section", "dp", None),
            P("section", "dp"),
        ),
        check_vma=False,
    )
```

```python
import functools

import jax
import jax.numpy as jnp
from jax import lax
from jax.experimental import pallas as pl
from jax.experimental.pallas import tpu as pltpu
from jax.sharding import PartitionSpec as P

F32 = jnp.float32
BF16 = jnp.bfloat16
SMALL = pl.CostEstimate(flops=0, bytes_accessed=0, transcendentals=0)
PARAMS = pltpu.CompilerParams(vmem_limit_bytes=56 * 1024 * 1024)


def partner(shard, axis, mask):
    length = lax.axis_size(axis)
    return lax.ppermute(shard, axis, [(i, i ^ mask) for i in range(length)])


def around(shard, axis, by):
    length = lax.axis_size(axis)
    return lax.ppermute(shard, axis, [(i, (i + by) % length) for i in range(length)])


def exchange_rows(block):
    length = lax.axis_size("tensor")
    if length == 4:
        return [block] + [partner(block, "tensor", r) for r in range(1, length)]
    return [block] + [around(block, "tensor", length - r) for r in range(1, length)]


def first_stage(block):
    if lax.axis_size("tensor") != 4:
        return exchange_rows(block)
    return [block, partner(block, "tensor", 1), partner(block, "tensor", 2)]


def second_stage(held, *before):
    if lax.axis_size("tensor") != 4:
        return held
    block, one, two = lax.optimization_barrier(tuple(held) + before)[:3]
    middle = lax.ppermute(block, "tensor", [(1, 2), (2, 1)])
    ends = lax.ppermute(two, "tensor", [(2, 3), (1, 0)])
    return [block, one, two, middle, ends]


def joined(held, *before):
    if len(held) == lax.axis_size("tensor"):
        return held
    block, one, two, middle, ends = held
    middle, ends = lax.optimization_barrier((middle, ends) + before)[:2]
    me = lax.axis_index("tensor")
    inside = (me == 1) | (me == 2)
    return [block, one, two, jnp.where(inside, middle, ends)]


def position(r):
    n = lax.axis_size("tensor")
    me = lax.axis_index("tensor")
    return me ^ r if n == 4 else (me + r) % n


def tied(value, *others):
    return lax.optimization_barrier((value,) + others)[0]


def chunks(width):
    step = min(width, 1024)
    return [slice(i, i + step) for i in range(0, width, step)]


def selected(routes_ref, count):
    ids = routes_ref[...]
    column = lax.broadcasted_iota(jnp.int32, (ids.shape[0], count), 1)
    return [(ids[:, k : k + 1] == column).astype(F32) for k in range(ids.shape[1])]


def probs_kernel(experts, hidden_ref, small_ref, routes_ref, probs_ref, inv_ref, marked_ref):
    width = hidden_ref.shape[1]
    square = jnp.zeros((hidden_ref.shape[0], 1), F32)
    for c in chunks(width):
        h = hidden_ref[:, c].astype(F32)
        square += jnp.sum(h * h, axis=1, keepdims=True)
    inv = 1.0 / jnp.sqrt(square / width + 1e-05)
    logits = jnp.zeros((hidden_ref.shape[0], small_ref.shape[0]), F32)
    for c in chunks(width):
        gain = small_ref[experts : experts + 1, c].astype(F32)
        normed = (hidden_ref[:, c].astype(F32) * inv * gain).astype(BF16)
        logits += lax.dot_general(
            normed, small_ref[:, c], (((1,), (1,)), ((), ())), preferred_element_type=F32
        )
    column = lax.broadcasted_iota(jnp.int32, logits.shape, 1)
    weights = jnp.where(column < experts, jnp.exp(jnp.where(column < experts, logits, 0.0)), 0.0)
    probs = weights / jnp.sum(weights, axis=1, keepdims=True)
    probs_ref[...] = probs
    inv_ref[...] = inv
    named = sum(selected(routes_ref, logits.shape[1]))
    marked_ref[...] = jnp.where(named > 0, probs, -1.0)


def step_kernel(experts, parts, kept, choose, flag_ref, *refs):
    refs = list(refs)
    up_ref = refs.pop(0)
    other_ref = refs.pop(0) if choose else None
    hidden_ref, out_ref, routes_ref, probs_ref, inv_ref, small_ref = refs[:6]
    back_refs, refs = refs[6 : 6 + parts], refs[6 + parts :]
    passed_ref, term_ref, norm_ref, upstream_ref = refs
    width = up_ref.shape[2]
    rows = up_ref.shape[1]
    cap = back_refs[0].shape[1]
    t = pl.program_id(0)

    @pl.when(t == 0)
    def _():
        term_ref[...] = jnp.zeros_like(term_ref)

    choice = selected(routes_ref.at[0], probs_ref.shape[2])
    named = sum(choice)
    row = lax.broadcasted_iota(jnp.int32, (rows, rows), 0)
    column = lax.broadcasted_iota(jnp.int32, (rows, rows), 1)
    place = jnp.dot(
        (column < row).astype(BF16), named.astype(BF16), preferred_element_type=F32
    )
    expert = lax.broadcasted_iota(jnp.int32, named.shape, 1)
    slot = lax.broadcasted_iota(jnp.int32, (rows, cap), 1).astype(F32)
    picks = []
    for i in range(parts):
        mine = expert == flag_ref[1 + i]
        is_named = jnp.sum(jnp.where(mine, named, 0.0), axis=1, keepdims=True)
        at = jnp.sum(jnp.where(mine, place, 0.0), axis=1, keepdims=True)
        picks.append(jnp.where((at == slot) & (is_named > 0), 1.0, 0.0))
    pick = jnp.concatenate(picks, axis=1).astype(BF16)

    score = [jnp.zeros((rows, 1), F32) for _ in choice]
    for c in chunks(width):
        up = up_ref[0, :, c].astype(F32)
        if choose:
            up = jnp.where(flag_ref[0] == 1, up, other_ref[0, :, c].astype(F32))
        upstream_ref[:, c] = up
        for k in range(len(choice)):
            out = out_ref[0, :, k * width + c.start : k * width + c.stop].astype(F32)
            score[k] += jnp.sum(up * out, axis=1, keepdims=True)
    prob_grad = sum(a * b for a, b in zip(score, choice))
    p = probs_ref[0]
    logit_grad = (p * (prob_grad - jnp.sum(p * prob_grad, axis=1, keepdims=True))).astype(BF16)
    inv = inv_ref[0]
    mean = jnp.zeros((rows, 1), F32)
    for c in chunks(width):
        norm = jnp.dot(logit_grad, small_ref[:, c], preferred_element_type=F32)
        back = jnp.concatenate([ref[0, :, c] for ref in back_refs], axis=0)
        norm += jnp.dot(pick, back, preferred_element_type=F32)
        norm_ref[:, c] = norm
        gain = small_ref[experts : experts + 1, c].astype(F32)
        mean += jnp.sum(norm * gain * hidden_ref[0, :, c].astype(F32), axis=1, keepdims=True)
    mean = mean / width
    for c in chunks(width):
        gain = small_ref[experts : experts + 1, c].astype(F32)
        h = hidden_ref[0, :, c].astype(F32)
        grad = inv * (norm_ref[:, c] * gain) - h * inv**3 * mean
        passed_ref[0, :, c] = (upstream_ref[:, c] + grad).astype(BF16)

    @pl.when(t < kept)
    def _():
        for c in chunks(width):
            gain = small_ref[experts : experts + 1, c].astype(F32)
            scaled = hidden_ref[0, :, c].astype(F32) * inv
            normed = (scaled * gain).astype(BF16)
            router = lax.dot_general(
                logit_grad, normed, (((0,), (0,)), ((), ())), preferred_element_type=F32
            )
            gains = jnp.sum(norm_ref[:, c] * scaled, axis=0, keepdims=True)
            line = lax.broadcasted_iota(jnp.int32, router.shape, 0)
            term_ref[:, c] += jnp.where(line == experts, gains, router)


def gate_kernel(order_ref, scan_ref, gate_ref, out_ref):
    for r in range(out_ref.shape[1]):
        gate = gate_ref[0, order_ref[r]].astype(F32)
        scan = scan_ref[0, order_ref[r]].astype(F32)
        out_ref[0, r] = (scan * gate * (1.0 / (1.0 + jnp.exp(-gate)))).astype(BF16)


def inner_kernel(n, order_ref, *refs):
    blocks = refs[: 2 * n]
    weight_ref, scan_ref, gate_ref, scan_out, gate_out, held = refs[2 * n :]
    rows = blocks[0].shape[1]
    group = n * rows

    @pl.when(pl.program_id(0) == 0)
    def _():
        for i, ref in enumerate(blocks):
            for t in range(ref.shape[0]):
                step = t if i < n else t + 1
                start = pl.multiple_of(step * group + order_ref[i % n] * rows, 16)
                held[pl.ds(start, rows), :] = ref[t]

    inner = lax.dot_general(
        held[...], weight_ref[...], (((1,), (1,)), ((), ())), preferred_element_type=F32
    )
    for t in range(scan_ref.shape[0]):
        part = inner[t * group : (t + 1) * group]
        gate = gate_ref[t].astype(F32)
        scan = scan_ref[t].astype(F32)
        sig = 1.0 / (1.0 + jnp.exp(-gate))
        scan_out[t] = (part * gate * sig).astype(BF16)
        gate_out[t] = (part * scan * sig * (1.0 + gate * (1.0 - sig))).astype(BF16)


def columns_kernel(n, *refs):
    blocks, out_ref = refs[:n], refs[-1]
    rows = blocks[0].shape[1]
    for t in range(blocks[0].shape[0]):
        for r, ref in enumerate(blocks):
            start = (t * n + r) * rows
            out_ref[0, start : start + rows, :] = ref[t]
    if len(refs) > n + 1:
        start = blocks[0].shape[0] * n * rows
        out_ref[0, start:, :] = (refs[n][...] + refs[n + 1][...]).astype(BF16)


def weight_kernel(order_ref, *refs):
    lefts, (first_ref, later_ref, out_ref, held) = refs[:-4], refs[-4:]
    groups, rows, _ = first_ref.shape
    depth = lefts[0].shape[0]

    @pl.when(pl.program_id(0) == 0)
    def _():
        for g in range(groups):
            start = pl.multiple_of(order_ref[g] * depth, 16)
            held[pl.ds(start, rows), :] = first_ref[g]
            start = pl.multiple_of(order_ref[g] * depth + rows, 16)
            held[pl.ds(start, depth - rows), :] = later_ref[g, : depth - rows, :]

    left = jnp.concatenate([ref[...] for ref in lefts], axis=0)
    out_ref[...] = lax.dot_general(
        left, held[...], (((0,), (0,)), ((), ())), preferred_element_type=F32
    )


def dispatch_kernel(n, order_ref, marks_ref, *refs):
    out_ref = refs[2 * n]
    _, rows, width = refs[0].shape
    cap = out_ref.shape[1] // n
    row = lax.broadcasted_iota(jnp.int32, (rows, rows), 0)
    column = lax.broadcasted_iota(jnp.int32, (rows, rows), 1)
    before = (row < column).astype(BF16)
    slot = lax.broadcasted_iota(jnp.int32, (cap, rows), 0).astype(F32)
    owner = lax.broadcasted_iota(jnp.int32, (n * cap, rows), 0) // cap
    puts, prob = [], 0.0
    for r in range(n):
        mark = marks_ref[0, r : r + 1, :]
        named = (mark >= 0).astype(F32)
        place = jnp.dot(named.astype(BF16), before, preferred_element_type=F32)
        put = jnp.where((slot == place) & (named > 0), 1.0, 0.0)
        put = jnp.where(owner == order_ref[r], jnp.concatenate([put] * n, axis=0), 0.0)
        prob += jnp.sum(put * mark, axis=1, keepdims=True)
        puts.append(put)
    put = jnp.concatenate(puts, axis=1).astype(BF16)

    def fill(sources):
        for c in chunks(width):
            source = jnp.concatenate([ref[0, :, c] for ref in sources], axis=0)
            moved = jnp.dot(put, source, preferred_element_type=F32)
            out_ref[0, :, c] = (prob * moved).astype(BF16)

    @pl.when(pl.program_id(0) == 0)
    def _():
        fill(refs[:n])

    @pl.when(pl.program_id(0) > 0)
    def _():
        fill(refs[n : 2 * n])


def whole_spec(array, extra=0):
    zeros = (0,) * array.ndim
    return pl.BlockSpec(array.shape, lambda *_: zeros, pipeline_mode=pl.Buffered(1))


def on_device(
    incoming, hidden, expert_out, routes, expert_back, scan_out, gate_in, w_out, w_router, norm_gain
):
    micro = incoming.shape[1]
    rows = incoming.shape[2]
    width = incoming.shape[3]
    experts = w_router.shape[2]
    n = lax.axis_size("tensor")
    n_dp = lax.axis_size("dp")
    cap = expert_back.shape[2] // n
    inner = scan_out.shape[3]
    group = scan_out.shape[2]
    columns = width // n_dp
    padded = -(-(experts + 1) // 16) * 16
    me = lax.axis_index("tensor")
    me_dp = lax.axis_index("dp")
    section = lax.axis_index("section")
    upper = section == 1
    order = jnp.stack([position(r) for r in range(n)]).astype(jnp.int32)
    weight = w_out[0]
    call = functools.partial(pl.pallas_call, compiler_params=PARAMS, cost_estimate=SMALL)

    back = expert_back[0].reshape(micro, n, cap, width)
    returned = [lax.dynamic_index_in_dim(back, me, 1, False)]
    for r in range(1, n):
        if n == 4:
            block = lax.dynamic_index_in_dim(back, me ^ r, 1, False)
            returned.append(partner(block, "tensor", r))
        else:
            block = lax.dynamic_index_in_dim(back, (me + n - r) % n, 1, False)
            returned.append(around(block, "tensor", n - r))

    small = jnp.concatenate([w_router[0].T, norm_gain[0][None]], axis=0)
    smalls = lax.all_gather(small, "dp", axis=1, tiled=True)
    smalls = jnp.pad(smalls, ((0, padded - experts - 1), (0, 0)))

    probs, inv_rms, marked = call(
        functools.partial(probs_kernel, experts),
        out_shape=(
            jax.ShapeDtypeStruct((micro * rows, padded), F32),
            jax.ShapeDtypeStruct((micro * rows, 1), F32),
            jax.ShapeDtypeStruct((micro * rows, padded), F32),
        ),
        name="probs",
    )(hidden[0].reshape(micro * rows, width), smalls, routes[0].reshape(micro * rows, -1))
    probs = probs.reshape(micro, rows, padded)
    inv_rms = inv_rms.reshape(micro, rows, 1)
    out_rows = expert_out[0].reshape(micro, rows, -1)
    flag = jnp.concatenate([section.astype(jnp.int32)[None], order])

    def step_back(t0, t1, kept, upstream, other=None):
        count = t1 - t0
        shifted = [hidden[0], out_rows, routes[0], probs, inv_rms]
        arrays, shift = [upstream], [t0]
        if other is not None:
            arrays, shift = arrays + [other], shift + [0]
        arrays, shift = arrays + shifted, shift + [t0] * len(shifted)
        specs = []
        for a, s in zip(arrays, shift):
            rest = (0,) * (a.ndim - 1)
            specs.append(
                pl.BlockSpec((1,) + a.shape[1:], lambda t, s=s, rest=rest: (t + s,) + rest)
            )
        arrays.append(smalls)
        specs.append(whole_spec(smalls))
        for a in returned:
            specs.append(pl.BlockSpec((1,) + a.shape[1:], lambda t: (t + t0, 0, 0)))
            arrays.append(a)
        return call(
            functools.partial(step_kernel, experts, len(returned), kept, other is not None),
            grid=(count,),
            out_shape=(
                jax.ShapeDtypeStruct((count, rows, width), BF16),
                jax.ShapeDtypeStruct((padded, width), F32),
            ),
            in_specs=[pl.BlockSpec(memory_space=pltpu.SMEM)] + specs,
            out_specs=(
                pl.BlockSpec((1, rows, width), lambda t: (t, 0, 0)),
                pl.BlockSpec((padded, width), lambda t: (0, 0)),
            ),
            scratch_shapes=[pltpu.VMEM((rows, width), F32)] * 2,
            name="step",
        )(flag, *arrays)

    four = (micro, n, rows, inner)
    spec = pl.BlockSpec((1, n, rows, inner), lambda t, o: (t, 0, 0, 0))
    gated = call(
        gate_kernel,
        out_shape=jax.ShapeDtypeStruct(four, BF16),
        grid_spec=pltpu.PrefetchScalarGridSpec(
            num_scalar_prefetch=1, grid=(micro,), in_specs=[spec] * 2, out_specs=spec
        ),
        name="gate",
    )(order, tied(scan_out[0].reshape(four), probs), gate_in[0].reshape(four))

    def columns_over(blocks, terms=()):
        count = blocks[0].shape[0]
        high = count * group + (padded if terms else 0)
        split = call(
            functools.partial(columns_kernel, n),
            grid=(n_dp,),
            out_shape=jax.ShapeDtypeStruct((n_dp, high, columns), BF16),
            in_specs=[pl.BlockSpec((count, rows, columns), lambda g: (0, 0, g))] * n
            + [pl.BlockSpec((padded, columns), lambda g: (0, g))] * len(terms),
            out_specs=pl.BlockSpec((1, high, columns), lambda g: (g, 0, 0)),
            name="columns",
        )(*blocks, *terms)
        return lax.all_to_all(split, "dp", split_axis=0, concat_axis=0, tiled=True)

    first, term_first = step_back(0, micro - 1, 1, tied(incoming[0], gated))
    received = lax.ppermute(first, "section", [(1, 0)])
    near_rows = exchange_rows(first[:1])

    gated = tied(gated.reshape(micro * group, inner), first)
    if n_dp == 4:
        across = partner(gated, "dp", 2)
        lefts = [gated, partner(gated, "dp", 1), across, partner(across, "dp", 1)]
    else:
        lefts = [gated] + [partner(gated, "dp", m) for m in range(1, n_dp)]


    later, term_later = step_back(
        1, micro, micro, incoming[0], received
    )
    passed_all = jnp.concatenate([first[:1], later], axis=0)
    far_half = first_stage(tied(later, *near_rows[1:]))
    far_rows = joined(second_stage(far_half, *lefts))
    across_first = columns_over([tied(near_rows[0], *far_half[1:])] + near_rows[1:])
    upstream = jnp.where(upper, incoming[0, 1:], received)
    source_first = joined(second_stage(first_stage(tied(incoming[0, :1], *far_half[1:]))))
    source_half = first_stage(tied(upstream, *source_first[1:]))
    rights = [across_first, columns_over(
        [tied(far_rows[0], across_first)] + far_rows[1:], (term_first, term_later)
    )]

    tile = min(inner, 256)
    blocks = near_rows + far_rows
    rows_spec = pl.BlockSpec((micro, group, tile), lambda i, o: (0, 0, i))
    scan_grad, gate_grad = call(
        functools.partial(inner_kernel, n),
        out_shape=[jax.ShapeDtypeStruct((micro, group, inner), BF16)] * 2,
        grid_spec=pltpu.PrefetchScalarGridSpec(
            num_scalar_prefetch=1,
            grid=(inner // tile,),
            in_specs=[whole_spec(b) for b in blocks]
            + [pl.BlockSpec((tile, width), lambda i, o: (i, 0))]
            + [rows_spec] * 2,
            out_specs=[rows_spec] * 2,
            scratch_shapes=[pltpu.VMEM((micro * group, width), BF16)],
        ),
        name="project",
    )(order, *blocks, weight, scan_out[0], gate_in[0])

    source_later = second_stage(source_half, scan_grad)
    depth = lefts[0].shape[0]
    order_dp = me_dp ^ jnp.arange(n_dp, dtype=jnp.int32)
    tile = min(inner, 512)
    weight_grad = call(
        weight_kernel,
        out_shape=jax.ShapeDtypeStruct((inner, columns), F32),
        grid_spec=pltpu.PrefetchScalarGridSpec(
            num_scalar_prefetch=1,
            grid=(inner // tile,),
            in_specs=[pl.BlockSpec((depth, tile), lambda i, o: (0, i))] * n_dp
            + [whole_spec(x) for x in rights],
            out_specs=pl.BlockSpec((tile, columns), lambda i, o: (i, 0)),
            scratch_shapes=[pltpu.VMEM((n_dp * depth, columns), BF16)],
        ),
        name="weight_grad",
    )(order_dp, *lefts, *rights)

    source_later = joined(source_later, weight_grad)
    total = jnp.sum(tied(rights[1], scan_grad)[:, -padded:].astype(F32), axis=0)[: experts + 1]
    marks = marked[:, :experts].T.reshape(1, -1)
    marks = jnp.pad(marks, ((0, 0), (0, -marks.shape[1] % columns))).reshape(-1, columns)
    shared = exchange_rows(jnp.concatenate([total, marks], axis=0))
    total = sum(x[: experts + 1] for x in shared)
    marks = jnp.concatenate([x[experts + 1 :] for x in shared], axis=0)
    marks = marks.reshape(n, -1)[:, : experts * micro * rows].reshape(n, experts, micro, rows)
    mine = jnp.swapaxes(lax.dynamic_index_in_dim(marks, me, 1, False), 0, 1)

    expert_grad = call(
        functools.partial(dispatch_kernel, n),
        out_shape=jax.ShapeDtypeStruct((micro, n * cap, width), BF16),
        grid_spec=pltpu.PrefetchScalarGridSpec(
            num_scalar_prefetch=1,
            grid=(micro,),
            in_specs=[pl.BlockSpec((1, n, rows), lambda t, o: (t, 0, 0))]
            + [whole_spec(x) for x in source_first]
            + [pl.BlockSpec((1, rows, width), lambda t, o: (jnp.maximum(t - 1, 0), 0, 0))] * n,
            out_specs=pl.BlockSpec((1, n * cap, width), lambda t, o: (t, 0, 0)),
        ),
        name="dispatch",
    )(order, mine, *source_first, *source_later)

    return (
        passed_all[None],
        scan_grad[None],
        gate_grad[None],
        expert_grad[None],
        weight_grad[None],
        total[:experts].T[None],
        total[experts][None],
    )


def solution(mesh):
    placed = (
        P("section", None, ("dp", "tensor"), None),
        P("section", None, ("dp", "tensor"), None),
        P("section", None, ("dp", "tensor"), None, None),
        P("section", None, ("dp", "tensor"), None),
        P("section", None, ("dp", "tensor"), None),
        P("section", None, "dp", "tensor"),
        P("section", None, "dp", "tensor"),
        P("section", "tensor", None),
        P("section", "dp", None),
        P("section", "dp"),
    )
    return jax.shard_map(
        on_device,
        mesh=mesh,
        in_specs=placed,
        out_specs=(
            P("section", None, ("dp", "tensor"), None),
            P("section", None, "dp", "tensor"),
            P("section", None, "dp", "tensor"),
            P("section", None, ("dp", "tensor"), None),
            P("section", "tensor", "dp"),
            P("section", "dp", None),
            P("section", "dp"),
        ),
        check_vma=False,
    )
```
